512 devices in a mesh: dp: 8 (over y_hi, x), ctx: 16 (over z, core), exp: 4 (over y_lo).
Axes of the slice: x: 4, y: 8 (y_hi: 2, y_lo: 4; y = y_hi * 4 + y_lo), z: 8, core: 2. Of those that a mesh axis runs over, the one named last changes fastest.
Arguments:
- queries: bfloat16 [16384, 4096], P(('dp', 'ctx'), 'exp'), may hold values from -4 to 4
- saved_key_rows: bfloat16 [16384, 256], P(('dp', 'ctx'), 'exp'), may hold values from -4 to 4
- saved_value_rows: bfloat16 [16384, 256], P(('dp', 'ctx'), 'exp'), may hold values from -6 to 6
- attn_out: bfloat16 [16384, 4096], P(('dp', 'ctx'), 'exp'), may hold values from -6 to 6
- log_sum_norm: float32 [64, 16384], P('exp', ('dp', 'ctx')), may hold values from 4 to 7
- grad_out: bfloat16 [16384, 4096], P(('dp', 'ctx'), 'exp'), may hold values from -6 to 6
- routes: int32 [16384, 2], P(('dp', 'ctx')), may hold values from 0 to 15, all different within a row; in each aligned block of 128 rows (0 to 127, 128 to 255, ...) at most 32 rows name the same one
- gates: float32 [16384, 2], P(('dp', 'ctx')), may hold values from 0.1 to 1
- expert_in: bfloat16 [8, 16, 512, 4096], P('dp', 'ctx', None, 'exp'), may hold values from -0.09375 to 0.09375
- hidden_grad: bfloat16 [8, 16, 512, 1536], P('dp', 'ctx'), may hold values from -6 to 6
- up_weight: bfloat16 [16, 1536, 4096], P('ctx', 'dp', 'exp'), may hold values from -0.15625 to 0.15625
Outputs:
- grad_hidden: bfloat16 [16384, 4096], P(('dp', 'ctx'), 'exp')
- query_gradient: bfloat16 [16384, 4096], P(('dp', 'ctx'), 'exp')
- key_gradient: bfloat16 [16384, 256], P(('dp', 'ctx'), 'exp')
- value_gradient: bfloat16 [16384, 256], P(('dp', 'ctx'), 'exp')
- grad_up: bfloat16 [16, 1536, 4096], P('ctx', 'dp', 'exp')
The draws below stay inside these ranges and needn't reach their ends.
Inputs may be any that keep to these rules, and one draw needn't show every extreme that they name: Each token names 2 different experts. Among the tokens of one device (an aligned block of 128 rows) no expert is named by more than 32 routes; some expert is named by exactly 32 routes in some blocks.
All inputs are finite; a program needn't handle non-finite values.
Results may differ from the reference program's by a relative error of at most 0.015.
Values may be sent and summed in bfloat16 or wider, within the bound.
No kernel may reach another device: no remote copies, remote signals or barrier semaphores. Data moves between devices by JAX's collectives and lax.ppermute only.
A program may use at most 128 MiB of HBM per device.

```python
import math
from functools import partial
import jax
import jax.numpy as jnp
import numpy as np
from jax import lax

D = 4096
FF = 1536
QUERY_HEADS = 64
KEY_VALUE_HEADS = 4
HEAD_WIDTH = 64
TOP = 2
TOK_DEV = 128
EXPERTS = 16
CAP = 32
SEQUENCE_LENGTH = 2048
TOKEN_COUNT = 16384
N_DP = 8
N_CTX = 16


def block_scale(key, shape, pieces, smallest, top_value):
    loudness = 1.0
    for dim, parts in pieces:
        heights = jax.random.uniform(jax.random.fold_in(jax.random.fold_in(key, 6), dim), (parts,), jnp.float32, smallest / len(pieces), top_value / len(pieces))
        loudness = loudness * jnp.repeat(jnp.exp(heights), shape[dim] // parts).reshape((-1,) + (1,) * (len(shape) - 1 - dim))
    return loudness


def shared_out(own_key, own, number, rows, amount, top, most, skew):
    order = jax.random.permutation(own_key, amount)
    heavy_load, usual = portions_of(amount, rows * top, most, skew, True), portions_of(amount, rows * top, most, skew, False)
    places = jnp.arange(amount)

    def named(tallies, offset_by):
        used = int((tallies > 0).sum())
        fixed = max(1, used // 4)
        moved = fixed + (places - fixed + offset_by * (used - fixed)) % max(1, amount - fixed)
        return jnp.zeros((amount,), jnp.int32).at[order[jnp.where(places < fixed, places, moved)]].set(jnp.asarray(tallies, jnp.int32))

    tallies = jnp.where(number % 4 == 0, named(heavy_load, number // 4), named(usual, number - number // 4 - 1))
    mixed = jax.random.permutation(jax.random.fold_in(own, 3), amount)
    source_of, taker = mixed[0:amount // 2 * 2:2], mixed[1:amount // 2 * 2:2]
    slack = jnp.minimum(tallies[source_of] - 1, most - tallies[taker]) // 2
    slack = jnp.where((source_of == order[0]) | (taker == order[0]) | (tallies[taker] == 0), 0, jnp.maximum(slack, 0))
    moved = jax.random.randint(jax.random.fold_in(own, 4), (amount // 2,), 0, 1 << 20) % (slack + 1)
    tallies = tallies.at[source_of].add(-moved).at[taker].add(moved)
    items = jnp.searchsorted(jnp.cumsum(tallies), jnp.arange(rows * top), side="right").astype(jnp.int32)
    table = items.reshape(top, rows).T
    table = table[jax.random.permutation(jax.random.fold_in(own, 1), rows)]
    offset_by = jax.random.randint(jax.random.fold_in(own, 2), (rows, 1), 0, top)
    return jnp.take_along_axis(table, (jnp.arange(top)[None, :] + offset_by) % top, axis=1)


def portions_of(count, total, limit, slope, full):
    portions = [(1 << 20) // math.isqrt(rank ** slope) + 1 for rank in range(1, count + 1)]
    largest = limit if full else min(limit, max(-(-total // count), total * portions[0] // sum(portions)))
    least = 1 if total - largest >= count - 1 else 0
    counts, spare = [largest] + [least] * (count - 1), total - largest - least * (count - 1)
    while spare > 0:
        candidates = [i for i in range(1, count) if counts[i] < largest] or [i for i in range(1, count) if counts[i] < limit]
        whole, budget = sum([portions[i] for i in candidates]), spare
        for i in candidates:
            more = min(limit - counts[i], max(1, budget * portions[i] // whole), spare)
            counts[i] = counts[i] + more
            spare = spare - more
    return np.array(counts)


def noise(stream_key, shape, width, reach, split=(), kind=jnp.bfloat16):
    values = jax.random.normal(stream_key, shape, jnp.float32) * width
    if len(split) > 0:
        values = block_scale(stream_key, shape, split, -0.22, 0.18) * values
    return jnp.clip(values, min=-reach, max=reach).astype(kind)


def setup_inputs(seed: int = 0) -> dict:
    streams_of = jax.random.split(jax.random.key(seed), 12)
    queries = noise(streams_of[0], (TOKEN_COUNT, QUERY_HEADS * HEAD_WIDTH), 1.0, 4.0, ((0, 128), (1, 4)))
    saved_key_rows = noise(streams_of[1], (TOKEN_COUNT, KEY_VALUE_HEADS * HEAD_WIDTH), 1.0, 4.0, ((0, 128), (1, 4)))
    saved_value_rows = noise(streams_of[2], (TOKEN_COUNT, KEY_VALUE_HEADS * HEAD_WIDTH), 1.0, 6.0, ((0, 128), (1, 4)))
    attn_out = noise(streams_of[3], (TOKEN_COUNT, QUERY_HEADS * HEAD_WIDTH), 1.0, 6.0, ((0, 128), (1, 4)))
    log_sum_norm = jnp.clip(4.0 + 3.0 * jax.random.uniform(streams_of[4], (QUERY_HEADS, TOKEN_COUNT), jnp.float32) ** block_scale(streams_of[4], (QUERY_HEADS, TOKEN_COUNT), ((0, 4), (1, 128)), -0.2, 0.2), 4.0, 7.0)
    grad_out = noise(streams_of[5], (TOKEN_COUNT, D), 1.0, 6.0, ((0, 128), (1, 4)))
    routes_keys = jax.random.split(jax.random.fold_in(streams_of[6], 1), TOKEN_COUNT // TOK_DEV)
    routes_turns = jax.random.permutation(jax.random.fold_in(streams_of[6], 3), TOKEN_COUNT // TOK_DEV)
    routes = jax.vmap(lambda own, number: shared_out(jax.random.fold_in(streams_of[6], 2), own, number, TOK_DEV, EXPERTS, TOP, CAP, 2))(routes_keys, routes_turns).reshape((TOKEN_COUNT, TOP))
    gates = jnp.clip(jnp.exp(math.log(1.0) - 2.3025851 * jax.random.uniform(streams_of[7], (TOKEN_COUNT, TOP), jnp.float32) ** block_scale(streams_of[7], (TOKEN_COUNT, TOP), ((0, 128),), -0.2, 0.2)), 0.1, 1.0)
    expert_in = noise(streams_of[8], (N_DP, EXPERTS, N_CTX * CAP, D), (N_DP * N_CTX * CAP) ** -0.5, 0.09375, ((0, 8), (1, 16), (3, 4)))
    hidden_grad = noise(streams_of[9], (N_DP, EXPERTS, N_CTX * CAP, FF), 1.0, 6.0, ((0, 8), (1, 16)))
    up_weight = noise(streams_of[10], (EXPERTS, FF, D), FF ** -0.5, 0.15625, ((0, 16), (1, 8), (2, 4)))
    return dict(queries=queries, saved_key_rows=saved_key_rows, saved_value_rows=saved_value_rows, attn_out=attn_out, log_sum_norm=log_sum_norm, grad_out=grad_out, routes=routes, gates=gates, expert_in=expert_in, hidden_grad=hidden_grad, up_weight=up_weight)


def slot_places(route_rows, experts):
    flat_routes = route_rows.reshape(-1)
    onehot = (flat_routes[:, None] == jnp.arange(experts, dtype=jnp.int32)[None, :]).astype(jnp.int32)
    before = jnp.cumsum(onehot, axis=0) - onehot
    return jnp.sum(before * onehot, axis=1).astype(jnp.int32)


def weight_partial(operands):
    return jnp.dot(operands[0].T, operands[1], preferred_element_type=jnp.float32).astype(jnp.bfloat16)


def expert_pass(operands):
    slot_grads, input_rows, weight = operands
    back_rows = jnp.dot(slot_grads.reshape(-1, FF), weight, preferred_element_type=jnp.float32)
    back_rows = back_rows.astype(jnp.bfloat16).reshape(N_DP, N_CTX * CAP, D)
    partials = lax.map(weight_partial, (slot_grads, input_rows))
    return back_rows, jnp.sum(partials.astype(jnp.float32), axis=0).astype(jnp.bfloat16)


def head_group(operands):
    query_rows, grad_heads, saved_out, norm_row_values, key_block, value_block = operands
    score_scale = HEAD_WIDTH ** -0.5
    query_f = query_rows.astype(jnp.float32)
    grad_f = grad_heads.astype(jnp.float32)
    key_f = key_block.astype(jnp.float32)
    value_f = value_block.astype(jnp.float32)
    row_delta = jnp.sum(grad_f * saved_out.astype(jnp.float32), axis=2).T
    scores = jnp.einsum("lgc,mc->glm", query_f, key_f) * score_scale
    positions = jnp.arange(query_rows.shape[0], dtype=jnp.int32)
    allowed = positions[None, :] <= positions[:, None]
    attend = jnp.where(allowed[None], jnp.exp(scores - norm_row_values[:, :, None]), 0.0)
    attend_b = lax.optimization_barrier(attend.astype(jnp.bfloat16)).astype(jnp.float32)
    value_grad_rows = jnp.einsum("glm,lgc->mc", attend_b, grad_f)
    prob_grad = jnp.einsum("lgc,mc->glm", grad_f, value_f)
    score_grad = attend * (prob_grad - row_delta[:, :, None])
    score_b = lax.optimization_barrier(score_grad.astype(jnp.bfloat16)).astype(jnp.float32)
    query_grad_rows = jnp.einsum("glm,mc->lgc", score_b, key_f) * score_scale
    key_grad_rows = jnp.einsum("glm,lgc->mc", score_b, query_f) * score_scale
    return query_grad_rows, key_grad_rows, value_grad_rows


def reference(queries, saved_key_rows, saved_value_rows, attn_out, log_sum_norm, grad_out, routes, gates, expert_in, hidden_grad, up_weight):
    blocks = routes.reshape(N_DP * N_CTX, TOK_DEV * TOP)
    places = jax.vmap(partial(slot_places, experts=EXPERTS))(blocks)
    back_rows, grad_up = lax.map(expert_pass, (hidden_grad.transpose(1, 0, 2, 3), expert_in.transpose(1, 0, 2, 3), up_weight))
    back_rows = back_rows.transpose(1, 0, 2, 3)
    route_ids = routes.reshape(N_DP, N_CTX, TOK_DEV * TOP)
    places = places.reshape(N_DP, N_CTX, TOK_DEV * TOP)
    row_index = jnp.arange(N_CTX, dtype=jnp.int32)[None, :, None] * CAP + places
    group_index = jnp.arange(N_DP, dtype=jnp.int32)[:, None, None]
    picked = back_rows[group_index, route_ids, row_index]
    weighted = picked.astype(jnp.float32).reshape(N_DP, N_CTX, TOK_DEV, TOP, D) * gates.reshape(N_DP, N_CTX, TOK_DEV, TOP)[..., None]
    grad_hidden = (grad_out.astype(jnp.float32) + jnp.sum(weighted, axis=3).reshape(TOKEN_COUNT, D)).astype(jnp.bfloat16)

    group_width = QUERY_HEADS // KEY_VALUE_HEADS

    def split_heads(array_operand):
        return array_operand.reshape(N_DP, SEQUENCE_LENGTH, KEY_VALUE_HEADS, group_width, HEAD_WIDTH).transpose(0, 2, 1, 3, 4).reshape(N_DP * KEY_VALUE_HEADS, SEQUENCE_LENGTH, group_width, HEAD_WIDTH)

    def split_kv(array_operand):
        return array_operand.reshape(N_DP, SEQUENCE_LENGTH, KEY_VALUE_HEADS, HEAD_WIDTH).transpose(0, 2, 1, 3).reshape(N_DP * KEY_VALUE_HEADS, SEQUENCE_LENGTH, HEAD_WIDTH)

    norm_row_values = log_sum_norm.reshape(KEY_VALUE_HEADS, group_width, N_DP, SEQUENCE_LENGTH).transpose(2, 0, 1, 3).reshape(N_DP * KEY_VALUE_HEADS, group_width, SEQUENCE_LENGTH)
    query_grad_rows, key_grad_rows, value_grad_rows = lax.map(head_group, (split_heads(queries), split_heads(grad_hidden), split_heads(attn_out), norm_row_values, split_kv(saved_key_rows), split_kv(saved_value_rows)))
    query_gradient = query_grad_rows.reshape(N_DP, KEY_VALUE_HEADS, SEQUENCE_LENGTH, group_width, HEAD_WIDTH).transpose(0, 2, 1, 3, 4).reshape(TOKEN_COUNT, QUERY_HEADS * HEAD_WIDTH).astype(jnp.bfloat16)
    key_gradient = key_grad_rows.reshape(N_DP, KEY_VALUE_HEADS, SEQUENCE_LENGTH, HEAD_WIDTH).transpose(0, 2, 1, 3).reshape(TOKEN_COUNT, KEY_VALUE_HEADS * HEAD_WIDTH).astype(jnp.bfloat16)
    value_gradient = value_grad_rows.reshape(N_DP, KEY_VALUE_HEADS, SEQUENCE_LENGTH, HEAD_WIDTH).transpose(0, 2, 1, 3).reshape(TOKEN_COUNT, KEY_VALUE_HEADS * HEAD_WIDTH).astype(jnp.bfloat16)
    return (grad_hidden, query_gradient, key_gradient, value_gradient, grad_up)
```

```python
import functools

import jax
import jax.numpy as jnp
from jax import lax
from jax.experimental import pallas as pl
from jax.experimental.pallas import tpu as pltpu
from jax.sharding import PartitionSpec as P

HEAD_WIDTH = 64
PAIR = 2 * HEAD_WIDTH
KEY_TILE = 256
ROW_TILE = 1024
QUERY_KEY_TILE = 512
QUERY_ROW_TILE = 512
X_RING = 4
F32 = jnp.float32
BF16 = jnp.bfloat16

NT = (((1,), (1,)), ((), ()))
TN = (((0,), (0,)), ((), ()))
LIGHT = pl.CostEstimate(flops=1 << 20, bytes_accessed=1 << 16, transcendentals=0)
X_GROUPS = [[0, 1, 2, 3], [4, 5, 6, 7]]


def other_y(shard):
    return lax.ppermute(shard, "dp", [(i, (i + X_RING) % (2 * X_RING)) for i in range(2 * X_RING)])


def along_x(shard, by):
    order = [(i, i // X_RING * X_RING + (i + by) % X_RING) for i in range(2 * X_RING)]
    return lax.ppermute(shard, "dp", order)


def run_copies(pairs, sems):
    copies = [pltpu.make_async_copy(src, dst, sems.at[i]) for i, (src, dst) in enumerate(pairs)]
    for copy in copies:
        copy.start()
    return copies


def repeat_kernel(shard_ref, out_ref):
    rows = shard_ref.shape[0]
    for i in range(X_RING):
        out_ref[i * rows : (i + 1) * rows, :] = shard_ref[...]


def repeated(shard):
    vmem = pl.BlockSpec(memory_space=pltpu.VMEM)
    return pl.pallas_call(
        repeat_kernel,
        out_shape=jax.ShapeDtypeStruct((X_RING * shard.shape[0], shard.shape[1]), shard.dtype),
        in_specs=[vmem],
        out_specs=vmem,
        cost_estimate=LIGHT,
        name="repeat",
    )(shard)


def over_x(shard):
    return lax.all_to_all(shard, "dp", 0, 0, tiled=True, axis_index_groups=X_GROUPS)


def back_kernel(line_ref, grads_ref, near_ref, far_ref, out_ref, grads, weight, sems):
    y = line_ref[0] // X_RING
    half = near_ref.shape[0]
    pairs = [(grads_ref, grads)]
    for ref, part in ((near_ref, y), (far_ref, 1 - y)):
        pairs.append((ref, weight.at[pl.ds(pl.multiple_of(part * half, half), half)]))
    for copy in run_copies(pairs, sems):
        copy.wait()
    width = out_ref.shape[1] // 2
    for i in range(2):
        at = slice(i * width, (i + 1) * width)
        out_ref[:, at] = jnp.dot(grads[...], weight[:, at], preferred_element_type=F32).astype(BF16)


def back_product(line, grads, near, far):
    depth, width = grads.shape[1], far.shape[1]
    anywhere = pl.BlockSpec(memory_space=pl.ANY)
    return pl.pallas_call(
        back_kernel,
        out_shape=jax.ShapeDtypeStruct((grads.shape[0], width), BF16),
        in_specs=[pl.BlockSpec(memory_space=pltpu.SMEM)] + [anywhere] * 3,
        out_specs=pl.BlockSpec(memory_space=pltpu.VMEM),
        scratch_shapes=[
            pltpu.VMEM(grads.shape, BF16),
            pltpu.VMEM((depth, width), BF16),
            pltpu.SemaphoreType.DMA((3,)),
        ],
        compiler_params=pltpu.CompilerParams(vmem_limit_bytes=32 * 2**20),
        cost_estimate=LIGHT,
        name="back_rows",
    )(line, grads, near, far)


def over_ctx(shard):
    return lax.all_to_all(shard, "ctx", 0, 0, tiled=True)


def swap_halves(pair):
    return pltpu.roll(pair, HEAD_WIDTH, 1)


def tile_rows(index, size):
    return pl.ds(pl.multiple_of(index * size, size), size)


def last_tile(place, size, tokens):
    return place * tokens // size


def per_head(pair, tokens):
    even = slice(2 * pair * tokens, (2 * pair + 1) * tokens)
    odd = slice((2 * pair + 1) * tokens, (2 * pair + 2) * tokens)
    return slice(pair * PAIR, (pair + 1) * PAIR), even, odd


def attend_kernel(place_ref, query_ref, norm_ref, kv_ref, attend_ref, low_ref, low, norm):
    tokens, width = query_ref.shape
    j, place = pl.program_id(0), place_ref[0]
    last = last_tile(place, KEY_TILE, tokens)

    @pl.when(j == 0)
    def _():
        first = lax.broadcasted_iota(jnp.int32, (tokens, PAIR), 1) < HEAD_WIDTH
        for pair in range(width // PAIR):
            columns, even, odd = per_head(pair, tokens)
            q = query_ref[:, columns].astype(F32) * (HEAD_WIDTH**-0.5)
            low[even, :] = jnp.where(first, q, 0.0).astype(BF16)
            low[odd, :] = jnp.where(first, swap_halves(q), 0.0).astype(BF16)
            norm[:, even] = norm_ref[2 * pair : 2 * pair + 1, :]
            norm[:, odd] = norm_ref[2 * pair + 1 : 2 * pair + 2, :]
        low_ref[...] = low[...]

    def tile(masked):
        kv = kv_ref[tile_rows(j, KEY_TILE), :]
        for r in range(low.shape[0] // ROW_TILE):
            at = slice(r * ROW_TILE, (r + 1) * ROW_TILE)
            scores = lax.dot_general(kv, low[at, :], NT, preferred_element_type=F32)
            attend = jnp.exp(scores - norm[:, at])
            if masked:
                key_pos = j * KEY_TILE + lax.broadcasted_iota(jnp.int32, attend.shape, 0)
                token = lax.broadcasted_iota(jnp.int32, attend.shape, 1) % tokens
                attend = jnp.where(key_pos <= place * tokens + token, attend, 0.0)
            attend_ref[:, at] = attend.astype(BF16)

    pl.when(j < last)(lambda: tile(False))
    pl.when(j == last)(lambda: tile(True))


def key_value_kernel(
    place_ref, mix_ref, rows_ref, grad_out_ref, out_ref, attend_ref, low_ref, kv_ref,
    hidden_ref, sum_ref, high, delta,
):
    tokens, width = grad_out_ref.shape
    j, place = pl.program_id(0), place_ref[0]
    last = last_tile(place, KEY_TILE, tokens)

    @pl.when(j == 0)
    def _():
        first = lax.broadcasted_iota(jnp.int32, (tokens, PAIR), 1) < HEAD_WIDTH
        mixed = jnp.dot(mix_ref[...], rows_ref[...], preferred_element_type=F32)
        hidden = (
            grad_out_ref[...].astype(F32)
            + (mixed[:tokens] + (mixed[tokens : 2 * tokens] + mixed[2 * tokens :]))
        ).astype(BF16)
        hidden_ref[...] = hidden
        for pair in range(width // PAIR):
            columns, even, odd = per_head(pair, tokens)
            g = hidden[:, columns].astype(F32)
            high[even, :] = jnp.where(first, 0.0, swap_halves(g)).astype(BF16)
            high[odd, :] = jnp.where(first, 0.0, g).astype(BF16)
            prod = (g * out_ref[:, columns].astype(F32)).T
            delta[:, even] = jnp.sum(prod[:HEAD_WIDTH], axis=0, keepdims=True)
            delta[:, odd] = jnp.sum(prod[HEAD_WIDTH:], axis=0, keepdims=True)

    @pl.when(j <= last)
    def _():
        kv = kv_ref[tile_rows(j, KEY_TILE), :]
        total = jnp.zeros((KEY_TILE, PAIR), F32)
        for r in range(high.shape[0] // ROW_TILE):
            at = slice(r * ROW_TILE, (r + 1) * ROW_TILE)
            g = high[at, :]
            attend = attend_ref[:, at]
            prob = lax.dot_general(kv, g, NT, preferred_element_type=F32)
            score_grad = (attend.astype(F32) * (prob - delta[:, at])).astype(BF16)
            total = total + jnp.dot(score_grad, low_ref[at, :], preferred_element_type=F32)
            total = total + jnp.dot(attend, g, preferred_element_type=F32)
        sum_ref[...] = total.astype(BF16)

    @pl.when(j > last)
    def _():
        sum_ref[...] = jnp.zeros_like(sum_ref)


def query_kernel(
    place_ref, hidden_ref, out_ref, low_ref, norm_ref, kv_ref, grad_ref, high, norm, delta, total
):
    tokens, width = hidden_ref.shape
    j, place = pl.program_id(0), place_ref[0]
    last = last_tile(place, QUERY_KEY_TILE, tokens)
    first = lax.broadcasted_iota(jnp.int32, (tokens, PAIR), 1) < HEAD_WIDTH

    @pl.when(j == 0)
    def _():
        norms = norm_ref[...].T
        for pair in range(width // PAIR):
            columns, even, odd = per_head(pair, tokens)
            g = hidden_ref[:, columns].astype(F32)
            high[even, :] = jnp.where(first, 0.0, swap_halves(g)).astype(BF16)
            high[odd, :] = jnp.where(first, 0.0, g).astype(BF16)
            prod = g * out_ref[:, columns].astype(F32)
            delta[even, :] = jnp.sum(jnp.where(first, prod, 0.0), axis=1, keepdims=True)
            delta[odd, :] = jnp.sum(jnp.where(first, 0.0, prod), axis=1, keepdims=True)
            norm[even, :] = norms[:, 2 * pair : 2 * pair + 1]
            norm[odd, :] = norms[:, 2 * pair + 1 : 2 * pair + 2]
        total[...] = jnp.zeros_like(total)

    def tile(masked):
        kv = kv_ref[tile_rows(j, QUERY_KEY_TILE), :]
        for r in range(high.shape[0] // QUERY_ROW_TILE):
            at = slice(r * QUERY_ROW_TILE, (r + 1) * QUERY_ROW_TILE)
            scores = lax.dot_general(low_ref[at, :], kv, NT, preferred_element_type=F32)
            attend = jnp.exp(scores - norm[at, :])
            if masked:
                key_pos = j * QUERY_KEY_TILE + lax.broadcasted_iota(jnp.int32, attend.shape, 1)
                token = lax.broadcasted_iota(jnp.int32, attend.shape, 0) % tokens
                attend = jnp.where(key_pos <= place * tokens + token, attend, 0.0)
            prob = lax.dot_general(high[at, :], kv, NT, preferred_element_type=F32)
            score_grad = (attend * (prob - delta[at, :])).astype(BF16)
            total[at, :] += jnp.dot(score_grad, kv, preferred_element_type=F32)

    pl.when(j < last)(lambda: tile(False))
    pl.when(j == last)(lambda: tile(True))

    @pl.when(j == pl.num_programs(0) - 1)
    def _():
        for pair in range(width // PAIR):
            columns, even, odd = per_head(pair, tokens)
            both = jnp.where(first, total[even, :], swap_halves(total[odd, :]))
            grad_ref[:, columns] = (both * (HEAD_WIDTH**-0.5)).astype(BF16)


def whole(array):
    return pl.BlockSpec(array.shape, lambda j, place: (0, 0))


def call(kernel, name, steps, in_specs, out_specs, out_shape, scratch, matmuls, elements, place, *operands):
    return pl.pallas_call(
        kernel,
        out_shape=out_shape,
        grid_spec=pltpu.PrefetchScalarGridSpec(
            num_scalar_prefetch=1,
            grid=(steps,),
            in_specs=in_specs,
            out_specs=out_specs,
            scratch_shapes=scratch,
        ),
        compiler_params=pltpu.CompilerParams(vmem_limit_bytes=60 * 2**20),
        cost_estimate=LIGHT,
        name=name,
    )(place, *operands)


def attend_block(tokens):
    return lambda j, place: (jnp.minimum(j, last_tile(place[0], KEY_TILE, tokens)), 0)


def attention_weights(place, queries, norms, kv):
    tokens, width = queries.shape
    keys, rows = kv.shape[0], width // HEAD_WIDTH * tokens
    out = (jax.ShapeDtypeStruct((keys, rows), BF16), jax.ShapeDtypeStruct((rows, PAIR), BF16))
    return call(
        attend_kernel,
        "attend",
        keys // KEY_TILE,
        [whole(queries), whole(norms), whole(kv)],
        (pl.BlockSpec((KEY_TILE, rows), attend_block(tokens)), whole(out[1])),
        out,
        [pltpu.VMEM((rows, PAIR), BF16), pltpu.VMEM((1, rows), F32)],
        1,
        keys * rows,
        place,
        queries,
        norms,
        kv,
    )


def key_value_grads(place, mix, rows, grad_out, attn_out, attend, low, kv):
    tokens, width = grad_out.shape
    keys, lines = attend.shape
    out = (jax.ShapeDtypeStruct((tokens, width), BF16), jax.ShapeDtypeStruct((keys, PAIR), BF16))
    return call(
        key_value_kernel,
        "key_value_grads",
        keys // KEY_TILE,
        [whole(mix), whole(rows), whole(grad_out), whole(attn_out)]
        + [pl.BlockSpec((KEY_TILE, lines), attend_block(tokens)), whole(low), whole(kv)],
        (whole(out[0]), pl.BlockSpec((KEY_TILE, PAIR), lambda j, place: (j, 0))),
        out,
        [pltpu.VMEM((lines, PAIR), BF16), pltpu.VMEM((1, lines), F32)],
        3,
        keys * lines,
        place,
        mix,
        rows,
        grad_out,
        attn_out,
        attend,
        low,
        kv,
    )


def query_grads(place, hidden, attn_out, low, norms, kv):
    keys, lines = kv.shape[0], low.shape[0]
    out = jax.ShapeDtypeStruct(hidden.shape, BF16)
    return call(
        query_kernel,
        "query_grads",
        keys // QUERY_KEY_TILE,
        [whole(x) for x in (hidden, attn_out, low, norms, kv)],
        whole(out),
        out,
        [
            pltpu.VMEM((lines, PAIR), BF16),
            pltpu.VMEM((lines, 1), F32),
            pltpu.VMEM((lines, 1), F32),
            pltpu.VMEM((lines, PAIR), F32),
        ],
        3,
        keys * lines,
        place,
        hidden,
        attn_out,
        low,
        norms,
        kv,
    )


def as_one(steps, step, *shapes):
    init = tuple(jnp.zeros(shape, BF16) for shape in shapes)
    return lax.fori_loop(0, steps, lambda i, carry: step(i.astype(jnp.int32)), init)


def pack_kernel(step_ref, key_ref, value_ref, kv_ref):
    del step_ref
    tokens = key_ref.shape[1]
    keys, values = key_ref[...].astype(F32).T.astype(BF16), value_ref[...].astype(F32).T.astype(BF16)
    for i in range(kv_ref.shape[0] // tokens):
        kv_ref[i * tokens : (i + 1) * tokens, :HEAD_WIDTH] = keys
        kv_ref[i * tokens : (i + 1) * tokens, HEAD_WIDTH:] = values


def over_chips(step, keys, values):
    chips = lax.axis_size("ctx") // 2
    vmem = pl.BlockSpec(memory_space=pltpu.VMEM)
    copies = pl.pallas_call(
        pack_kernel,
        out_shape=jax.ShapeDtypeStruct((chips * keys.shape[0], PAIR), BF16),
        in_specs=[pl.BlockSpec(memory_space=pltpu.SMEM)] + [vmem] * 2,
        out_specs=vmem,
        cost_estimate=LIGHT,
        name="pack",
    )(step.reshape(1), keys.T, values.T)
    same_core = [[2 * i + core for i in range(chips)] for core in range(2)]
    return lax.all_to_all(copies, "ctx", 0, 0, tiled=True, axis_index_groups=same_core)


def with_other_core(mine):
    devices = lax.axis_size("ctx")
    theirs = lax.ppermute(mine, "ctx", [(i, i ^ 1) for i in range(devices)])
    first = lax.axis_index("ctx") % 2 == 0
    parts = [x.reshape(devices // 2, -1, PAIR) for x in (mine, theirs)]
    both = jnp.stack([jnp.where(first, parts[0], parts[1]), jnp.where(first, parts[1], parts[0])], axis=1)
    return both.reshape(2 * mine.shape[0], PAIR)


def sum_kernel(parts_ref, key_ref, value_ref):
    total = jnp.sum(parts_ref[...].astype(F32), axis=0).T
    key_ref[...] = total[:HEAD_WIDTH].astype(BF16)
    value_ref[...] = total[HEAD_WIDTH:].astype(BF16)


def sum_parts(parts):
    vmem = pl.BlockSpec(memory_space=pltpu.VMEM)
    out = jax.ShapeDtypeStruct((HEAD_WIDTH, parts.shape[1]), BF16)
    keys, values = pl.pallas_call(
        sum_kernel,
        out_shape=(out, out),
        in_specs=[vmem],
        out_specs=(vmem, vmem),
        cost_estimate=LIGHT,
        name="sum_parts",
    )(parts)
    return keys.T, values.T


def mix_matrix(routes, gates, experts, capacity):
    tokens, top = routes.shape
    flat = routes.reshape(-1)
    number = jnp.arange(flat.shape[0], dtype=jnp.int32)
    same = (flat[:, None] == flat[None, :]) & (number[None, :] < number[:, None])
    slots = (flat * capacity + jnp.sum(same.astype(jnp.int32), axis=1)).reshape(tokens, top)
    terms, left = [], gates
    for _ in range(3):
        term = left.astype(BF16)
        left = left - term.astype(F32)
        terms.append(term)
    columns = jnp.arange(experts * capacity, dtype=jnp.int32)
    hit = slots[:, :, None] == columns[None, None, :]
    return jnp.concatenate(
        [sum(jnp.where(hit[:, k], t[:, k, None], 0).astype(BF16) for k in range(top)) for t in terms], axis=0
    )


def body(
    queries,
    saved_key_rows,
    saved_value_rows,
    attn_out,
    log_sum_norm,
    grad_out,
    routes,
    gates,
    expert_in,
    hidden_grad,
    up_weight,
):
    experts = lax.axis_size("ctx")
    place = lax.axis_index("ctx").astype(jnp.int32).reshape(1)
    line = lax.axis_index("dp")
    x, y = line % X_RING, line // X_RING
    tokens, width = queries.shape
    capacity = hidden_grad.shape[2] // experts
    weight = up_weight[0]
    shard_rows = weight.shape[0]
    half_rows = X_RING * shard_rows

    steps = 1 - place[0] // experts
    keys, pairs = experts * tokens, width // HEAD_WIDTH * tokens

    crossed = other_y(weight)
    near = lax.all_gather(weight, "dp", axis=0, tiled=True, axis_index_groups=X_GROUPS)

    chips = experts // 2
    (kv,) = as_one(
        steps, lambda i: (over_chips(i, saved_key_rows, saved_value_rows),), (chips * tokens, PAIR)
    )
    crossed, kv, routes = lax.optimization_barrier((crossed, kv, routes))
    kv = with_other_core(kv)
    copies = repeated(crossed)
    copies, slot_grads, inputs = lax.optimization_barrier((copies, hidden_grad[0, 0], expert_in[0, 0]))
    far = over_x(copies)

    def weight_term(half):
        grads = lax.dynamic_slice_in_dim(slot_grads, half * half_rows, half_rows, 1)
        return lax.dot_general(grads, inputs, TN, preferred_element_type=F32).astype(BF16)

    def x_sum(term):
        return lax.psum_scatter(term, "dp", scatter_dimension=0, tiled=True, axis_index_groups=X_GROUPS)

    attend, low = attention_weights(place, queries, log_sum_norm, kv)
    far, attend, low, term_far, term_near = lax.optimization_barrier(
        (far, attend, low, weight_term(1 - y), weight_term(y))
    )
    sum_far = x_sum(term_far)
    sum_near = x_sum(term_near)
    rows = over_ctx(back_product(line.astype(jnp.int32).reshape(1), slot_grads, near, far))
    mix = mix_matrix(routes, gates, experts, capacity)

    sum_far = other_y(sum_far)

    def attention(i):
        grad_hidden, total = key_value_grads(place + i, mix, rows, grad_out, attn_out, attend, low, kv)
        parts = over_ctx(total)
        query_gradient = query_grads(place + i, grad_hidden, attn_out, low, log_sum_norm, kv)
        return grad_hidden, query_gradient, parts

    grad_hidden, query_gradient, parts = as_one(
        steps, attention, (tokens, width), (tokens, width), (keys, PAIR)
    )
    key_gradient, value_gradient = sum_parts(parts.reshape(experts, tokens, PAIR))
    grad_up = (sum_near.astype(F32) + sum_far.astype(F32)).astype(BF16).reshape(up_weight.shape)
    return grad_hidden, query_gradient, key_gradient, value_gradient, grad_up


def solution(mesh):
    placed = (
        P(("dp", "ctx"), "exp"),
        P(("dp", "ctx"), "exp"),
        P(("dp", "ctx"), "exp"),
        P(("dp", "ctx"), "exp"),
        P("exp", ("dp", "ctx")),
        P(("dp", "ctx"), "exp"),
        P(("dp", "ctx"), None),
        P(("dp", "ctx"), None),
        P("dp", "ctx", None, "exp"),
        P("dp", "ctx", None, None),
        P("ctx", "dp", "exp"),
    )
    return jax.shard_map(
        body,
        mesh=mesh,
        in_specs=placed,
        out_specs=(
            P(("dp", "ctx"), "exp"),
            P(("dp", "ctx"), "exp"),
            P(("dp", "ctx"), "exp"),
            P(("dp", "ctx"), "exp"),
            P("ctx", "dp", "exp"),
        ),
        check_vma=False,
    )
```

```python
import functools

import jax
import jax.numpy as jnp
from jax import lax
from jax.experimental import pallas as pl
from jax.experimental.pallas import tpu as pltpu
from jax.sharding import PartitionSpec as P

HEAD_WIDTH = 64
PAIR = 2 * HEAD_WIDTH
KEY_TILE = 256
ROW_TILE = 1024
QUERY_KEY_TILE = 512
QUERY_ROW_TILE = 512
X_RING = 4
F32 = jnp.float32
BF16 = jnp.bfloat16

NT = (((1,), (1,)), ((), ()))
TN = (((0,), (0,)), ((), ()))
LIGHT = pl.CostEstimate(flops=1 << 20, bytes_accessed=1 << 16, transcendentals=0)
X_GROUPS = [[0, 1, 2, 3], [4, 5, 6, 7]]


def other_y(shard):
    return lax.ppermute(shard, "dp", [(i, (i + X_RING) % (2 * X_RING)) for i in range(2 * X_RING)])


def run_copies(pairs, sems):
    copies = [pltpu.make_async_copy(src, dst, sems.at[i]) for i, (src, dst) in enumerate(pairs)]
    for copy in copies:
        copy.start()
    return copies


def along_x(shard, by):
    order = [(i, i // X_RING * X_RING + (i + by) % X_RING) for i in range(2 * X_RING)]
    return lax.ppermute(shard, "dp", order)


def x_pieces(shard):
    return [shard] + [along_x(shard, by) for by in range(1, X_RING)]


def back_kernel(line_ref, grads_ref, near_ref, *rest):
    far, (out_ref, grads, weight, back, sems) = rest[:X_RING], rest[X_RING:]
    x, y = line_ref[0] % X_RING, line_ref[0] // X_RING
    half, rows = near_ref.shape[0], far[0].shape[0]
    near_rows = pl.ds(pl.multiple_of(y * half, half), half)
    pairs = [(grads_ref, grads), (near_ref, weight.at[near_rows])]
    for by, ref in enumerate(far):
        start = (1 - y) * half + (x + X_RING - by) % X_RING * rows
        pairs.append((ref, weight.at[pl.ds(pl.multiple_of(start, rows), rows)]))
    for copy in run_copies(pairs, sems):
        copy.wait()
    parts = sems.shape[0] - len(pairs)
    width = out_ref.shape[1] // parts
    copies = []
    for i in range(parts):
        at = slice(i * width, (i + 1) * width)
        back[:, at] = jnp.dot(grads[...], weight[:, at], preferred_element_type=F32).astype(BF16)
        copies.append(pltpu.make_async_copy(back.at[:, at], out_ref.at[:, at], sems.at[len(pairs) + i]))
        copies[-1].start()
    for copy in copies:
        copy.wait()


def back_product(line, grads, near, far):
    depth, width = grads.shape[1], near.shape[1]
    anywhere = pl.BlockSpec(memory_space=pl.ANY)
    return pl.pallas_call(
        back_kernel,
        out_shape=jax.ShapeDtypeStruct((grads.shape[0], width), BF16),
        in_specs=[pl.BlockSpec(memory_space=pltpu.SMEM)] + [anywhere] * (2 + X_RING),
        out_specs=anywhere,
        scratch_shapes=[
            pltpu.VMEM(grads.shape, BF16),
            pltpu.VMEM((depth, width), BF16),
            pltpu.VMEM((grads.shape[0], width), BF16),
            pltpu.SemaphoreType.DMA((2 + X_RING + 4,)),
        ],
        compiler_params=pltpu.CompilerParams(vmem_limit_bytes=60 * 2**20),
        cost_estimate=LIGHT,
        name="back_rows",
    )(line, grads, near, *far)


def over_ctx(shard):
    return lax.all_to_all(shard, "ctx", 0, 0, tiled=True)


def swap_halves(pair):
    return pltpu.roll(pair, HEAD_WIDTH, 1)


def tile_rows(index, size):
    return pl.ds(pl.multiple_of(index * size, size), size)


def last_tile(place, size, tokens):
    return place * tokens // size


def per_head(pair, tokens):
    even = slice(2 * pair * tokens, (2 * pair + 1) * tokens)
    odd = slice((2 * pair + 1) * tokens, (2 * pair + 2) * tokens)
    return slice(pair * PAIR, (pair + 1) * PAIR), even, odd


def attend_kernel(place_ref, query_ref, norm_ref, kv_ref, attend_ref, low_ref, low, norm):
    tokens, width = query_ref.shape
    j, place = pl.program_id(0), place_ref[0]
    last = last_tile(place, KEY_TILE, tokens)

    @pl.when(j == 0)
    def _():
        first = lax.broadcasted_iota(jnp.int32, (tokens, PAIR), 1) < HEAD_WIDTH
        for pair in range(width // PAIR):
            columns, even, odd = per_head(pair, tokens)
            q = query_ref[:, columns].astype(F32) * (HEAD_WIDTH**-0.5)
            low[even, :] = jnp.where(first, q, 0.0).astype(BF16)
            low[odd, :] = jnp.where(first, swap_halves(q), 0.0).astype(BF16)
            norm[:, even] = norm_ref[2 * pair : 2 * pair + 1, :]
            norm[:, odd] = norm_ref[2 * pair + 1 : 2 * pair + 2, :]
        low_ref[...] = low[...]

    def tile(masked):
        kv = kv_ref[tile_rows(j, KEY_TILE), :]
        for r in range(low.shape[0] // ROW_TILE):
            at = slice(r * ROW_TILE, (r + 1) * ROW_TILE)
            scores = lax.dot_general(kv, low[at, :], NT, preferred_element_type=F32)
            attend = jnp.exp(scores - norm[:, at])
            if masked:
                key_pos = j * KEY_TILE + lax.broadcasted_iota(jnp.int32, attend.shape, 0)
                token = lax.broadcasted_iota(jnp.int32, attend.shape, 1) % tokens
                attend = jnp.where(key_pos <= place * tokens + token, attend, 0.0)
            attend_ref[:, at] = attend.astype(BF16)

    pl.when(j < last)(lambda: tile(False))
    pl.when(j == last)(lambda: tile(True))


def key_value_kernel(
    place_ref, mix_ref, rows_ref, grad_out_ref, out_ref, attend_ref, low_ref, kv_ref,
    hidden_ref, sum_ref, high, delta,
):
    tokens, width = grad_out_ref.shape
    j, place = pl.program_id(0), place_ref[0]
    last = last_tile(place, KEY_TILE, tokens)

    @pl.when(j == 0)
    def _():
        first = lax.broadcasted_iota(jnp.int32, (tokens, PAIR), 1) < HEAD_WIDTH
        mixed = jnp.dot(mix_ref[...], rows_ref[...], preferred_element_type=F32)
        hidden = (
            grad_out_ref[...].astype(F32)
            + (mixed[:tokens] + (mixed[tokens : 2 * tokens] + mixed[2 * tokens :]))
        ).astype(BF16)
        hidden_ref[...] = hidden
        for pair in range(width // PAIR):
            columns, even, odd = per_head(pair, tokens)
            g = hidden[:, columns].astype(F32)
            high[even, :] = jnp.where(first, 0.0, swap_halves(g)).astype(BF16)
            high[odd, :] = jnp.where(first, 0.0, g).astype(BF16)
            prod = (g * out_ref[:, columns].astype(F32)).T
            delta[:, even] = jnp.sum(prod[:HEAD_WIDTH], axis=0, keepdims=True)
            delta[:, odd] = jnp.sum(prod[HEAD_WIDTH:], axis=0, keepdims=True)

    @pl.when(j <= last)
    def _():
        kv = kv_ref[tile_rows(j, KEY_TILE), :]
        total = jnp.zeros((KEY_TILE, PAIR), F32)
        for r in range(high.shape[0] // ROW_TILE):
            at = slice(r * ROW_TILE, (r + 1) * ROW_TILE)
            g = high[at, :]
            attend = attend_ref[:, at]
            prob = lax.dot_general(kv, g, NT, preferred_element_type=F32)
            score_grad = (attend.astype(F32) * (prob - delta[:, at])).astype(BF16)
            total = total + jnp.dot(score_grad, low_ref[at, :], preferred_element_type=F32)
            total = total + jnp.dot(attend, g, preferred_element_type=F32)
        sum_ref[...] = total.astype(BF16)

    @pl.when(j > last)
    def _():
        sum_ref[...] = jnp.zeros_like(sum_ref)


def query_kernel(
    place_ref, hidden_ref, out_ref, low_ref, norm_ref, kv_ref, grad_ref, high, norm, delta, total
):
    tokens, width = hidden_ref.shape
    j, place = pl.program_id(0), place_ref[0]
    last = last_tile(place, QUERY_KEY_TILE, tokens)
    first = lax.broadcasted_iota(jnp.int32, (tokens, PAIR), 1) < HEAD_WIDTH

    @pl.when(j == 0)
    def _():
        norms = norm_ref[...].T
        for pair in range(width // PAIR):
            columns, even, odd = per_head(pair, tokens)
            g = hidden_ref[:, columns].astype(F32)
            high[even, :] = jnp.where(first, 0.0, swap_halves(g)).astype(BF16)
            high[odd, :] = jnp.where(first, 0.0, g).astype(BF16)
            prod = g * out_ref[:, columns].astype(F32)
            delta[even, :] = jnp.sum(jnp.where(first, prod, 0.0), axis=1, keepdims=True)
            delta[odd, :] = jnp.sum(jnp.where(first, 0.0, prod), axis=1, keepdims=True)
            norm[even, :] = norms[:, 2 * pair : 2 * pair + 1]
            norm[odd, :] = norms[:, 2 * pair + 1 : 2 * pair + 2]
        total[...] = jnp.zeros_like(total)

    def tile(masked):
        kv = kv_ref[tile_rows(j, QUERY_KEY_TILE), :]
        for r in range(high.shape[0] // QUERY_ROW_TILE):
            at = slice(r * QUERY_ROW_TILE, (r + 1) * QUERY_ROW_TILE)
            scores = lax.dot_general(low_ref[at, :], kv, NT, preferred_element_type=F32)
            attend = jnp.exp(scores - norm[at, :])
            if masked:
                key_pos = j * QUERY_KEY_TILE + lax.broadcasted_iota(jnp.int32, attend.shape, 1)
                token = lax.broadcasted_iota(jnp.int32, attend.shape, 0) % tokens
                attend = jnp.where(key_pos <= place * tokens + token, attend, 0.0)
            prob = lax.dot_general(high[at, :], kv, NT, preferred_element_type=F32)
            score_grad = (attend * (prob - delta[at, :])).astype(BF16)
            total[at, :] += jnp.dot(score_grad, kv, preferred_element_type=F32)

    pl.when(j < last)(lambda: tile(False))
    pl.when(j == last)(lambda: tile(True))

    @pl.when(j == pl.num_programs(0) - 1)
    def _():
        for pair in range(width // PAIR):
            columns, even, odd = per_head(pair, tokens)
            both = jnp.where(first, total[even, :], swap_halves(total[odd, :]))
            grad_ref[:, columns] = (both * (HEAD_WIDTH**-0.5)).astype(BF16)


def whole(array):
    return pl.BlockSpec(array.shape, lambda j, place: (0, 0))


def call(kernel, name, steps, in_specs, out_specs, out_shape, scratch, matmuls, elements, place, *operands):
    return pl.pallas_call(
        kernel,
        out_shape=out_shape,
        grid_spec=pltpu.PrefetchScalarGridSpec(
            num_scalar_prefetch=1,
            grid=(steps,),
            in_specs=in_specs,
            out_specs=out_specs,
            scratch_shapes=scratch,
        ),
        compiler_params=pltpu.CompilerParams(vmem_limit_bytes=60 * 2**20),
        cost_estimate=LIGHT,
        name=name,
    )(place, *operands)


def attend_block(tokens):
    return lambda j, place: (jnp.minimum(j, last_tile(place[0], KEY_TILE, tokens)), 0)


def attention_weights(place, queries, norms, kv):
    tokens, width = queries.shape
    keys, rows = kv.shape[0], width // HEAD_WIDTH * tokens
    out = (jax.ShapeDtypeStruct((keys, rows), BF16), jax.ShapeDtypeStruct((rows, PAIR), BF16))
    return call(
        attend_kernel,
        "attend",
        keys // KEY_TILE,
        [whole(queries), whole(norms), whole(kv)],
        (pl.BlockSpec((KEY_TILE, rows), attend_block(tokens)), whole(out[1])),
        out,
        [pltpu.VMEM((rows, PAIR), BF16), pltpu.VMEM((1, rows), F32)],
        1,
        keys * rows,
        place,
        queries,
        norms,
        kv,
    )


def key_value_grads(place, mix, rows, grad_out, attn_out, attend, low, kv):
    tokens, width = grad_out.shape
    keys, lines = attend.shape
    out = (jax.ShapeDtypeStruct((tokens, width), BF16), jax.ShapeDtypeStruct((keys, PAIR), BF16))
    return call(
        key_value_kernel,
        "key_value_grads",
        keys // KEY_TILE,
        [whole(mix), whole(rows), whole(grad_out), whole(attn_out)]
        + [pl.BlockSpec((KEY_TILE, lines), attend_block(tokens)), whole(low), whole(kv)],
        (whole(out[0]), pl.BlockSpec((KEY_TILE, PAIR), lambda j, place: (j, 0))),
        out,
        [pltpu.VMEM((lines, PAIR), BF16), pltpu.VMEM((1, lines), F32)],
        3,
        keys * lines,
        place,
        mix,
        rows,
        grad_out,
        attn_out,
        attend,
        low,
        kv,
    )


def query_grads(place, hidden, attn_out, low, norms, kv):
    keys, lines = kv.shape[0], low.shape[0]
    out = jax.ShapeDtypeStruct(hidden.shape, BF16)
    return call(
        query_kernel,
        "query_grads",
        keys // QUERY_KEY_TILE,
        [whole(x) for x in (hidden, attn_out, low, norms, kv)],
        whole(out),
        out,
        [
            pltpu.VMEM((lines, PAIR), BF16),
            pltpu.VMEM((lines, 1), F32),
            pltpu.VMEM((lines, 1), F32),
            pltpu.VMEM((lines, PAIR), F32),
        ],
        3,
        keys * lines,
        place,
        hidden,
        attn_out,
        low,
        norms,
        kv,
    )


def as_one(always, step, *operands):
    out = jax.eval_shape(step, *operands)

    def never(*_):
        return jax.tree.map(lambda x: jnp.zeros(x.shape, x.dtype), out)

    return lax.cond(always, step, never, *operands)


def pack_kernel(key_ref, value_ref, kv_ref):
    tokens = key_ref.shape[1]
    keys, values = key_ref[...].astype(F32).T.astype(BF16), value_ref[...].astype(F32).T.astype(BF16)
    for i in range(kv_ref.shape[0] // tokens):
        kv_ref[i * tokens : (i + 1) * tokens, :HEAD_WIDTH] = keys
        kv_ref[i * tokens : (i + 1) * tokens, HEAD_WIDTH:] = values


def packed(keys, values):
    chips = lax.axis_size("ctx") // 2
    vmem = pl.BlockSpec(memory_space=pltpu.VMEM)
    return pl.pallas_call(
        pack_kernel,
        out_shape=jax.ShapeDtypeStruct((chips * keys.shape[0], PAIR), BF16),
        in_specs=[vmem] * 2,
        out_specs=vmem,
        cost_estimate=LIGHT,
        name="pack",
    )(keys.T, values.T)


def over_chips(copies):
    chips = lax.axis_size("ctx") // 2
    same_core = [[2 * i + core for i in range(chips)] for core in range(2)]
    return lax.all_to_all(copies, "ctx", 0, 0, tiled=True, axis_index_groups=same_core)


def with_other_core(mine):
    devices = lax.axis_size("ctx")
    theirs = lax.ppermute(mine, "ctx", [(i, i ^ 1) for i in range(devices)])
    first = lax.axis_index("ctx") % 2 == 0
    parts = [x.reshape(devices // 2, -1, PAIR) for x in (mine, theirs)]
    both = jnp.stack([jnp.where(first, parts[0], parts[1]), jnp.where(first, parts[1], parts[0])], axis=1)
    return both.reshape(2 * mine.shape[0], PAIR)


def sum_kernel(parts_ref, near_ref, far_ref, key_ref, value_ref, up_ref):
    total = jnp.sum(parts_ref[...].astype(F32), axis=0).T
    key_ref[...] = total[:HEAD_WIDTH].astype(BF16)
    value_ref[...] = total[HEAD_WIDTH:].astype(BF16)
    up_ref[...] = (near_ref[...].astype(F32) + far_ref[...].astype(F32)).astype(BF16)


def final_sums(parts, near, far):
    vmem = pl.BlockSpec(memory_space=pltpu.VMEM)
    out = jax.ShapeDtypeStruct((HEAD_WIDTH, parts.shape[1]), BF16)
    keys, values, up = pl.pallas_call(
        sum_kernel,
        out_shape=(out, out, jax.ShapeDtypeStruct(near.shape, BF16)),
        in_specs=[vmem] * 3,
        out_specs=(vmem,) * 3,
        compiler_params=pltpu.CompilerParams(vmem_limit_bytes=60 * 2**20),
        cost_estimate=LIGHT,
        name="final_sums",
    )(parts, near, far)
    return keys.T, values.T, up


def mix_matrix(routes, gates, experts, capacity):
    tokens, top = routes.shape
    flat = routes.reshape(-1)
    number = jnp.arange(flat.shape[0], dtype=jnp.int32)
    same = (flat[:, None] == flat[None, :]) & (number[None, :] < number[:, None])
    slots = (flat * capacity + jnp.sum(same.astype(jnp.int32), axis=1)).reshape(tokens, top)
    terms, left = [], gates
    for _ in range(3):
        term = left.astype(BF16)
        left = left - term.astype(F32)
        terms.append(term)
    columns = jnp.arange(experts * capacity, dtype=jnp.int32)
    hit = slots[:, :, None] == columns[None, None, :]
    return jnp.concatenate(
        [sum(jnp.where(hit[:, k], t[:, k, None], 0).astype(BF16) for k in range(top)) for t in terms], axis=0
    )


def body(
    queries,
    saved_key_rows,
    saved_value_rows,
    attn_out,
    log_sum_norm,
    grad_out,
    routes,
    gates,
    expert_in,
    hidden_grad,
    up_weight,
):
    experts = lax.axis_size("ctx")
    place = lax.axis_index("ctx").astype(jnp.int32).reshape(1)
    line = lax.axis_index("dp")
    x, y = line % X_RING, line // X_RING
    tokens, width = queries.shape
    capacity = hidden_grad.shape[2] // experts
    weight = up_weight[0]
    shard_rows = weight.shape[0]
    half_rows = X_RING * shard_rows

    always = place[0] < experts

    crossed = other_y(weight)
    near = lax.all_gather(weight, "dp", axis=0, tiled=True, axis_index_groups=X_GROUPS)
    slot_grads = hidden_grad[0, 0]

    def first(keys, values, grads, inputs):
        def weight_term(half):
            part = lax.dynamic_slice_in_dim(grads, half * half_rows, half_rows, 1)
            return lax.dot_general(part, inputs, TN, preferred_element_type=F32).astype(BF16)

        return packed(keys, values), weight_term(1 - y), weight_term(y)

    kv, term_far, term_near = as_one(
        always, first, saved_key_rows, saved_value_rows, slot_grads, expert_in[0, 0]
    )
    kv = over_chips(kv)
    crossed, routes, term_far, term_near = lax.optimization_barrier((crossed, routes, term_far, term_near))
    far = x_pieces(crossed)

    def second(kv, queries, norms):
        kv = with_other_core(kv)
        return kv, *attention_weights(place, queries, norms, kv)

    kv, attend, low = as_one(always, second, kv, queries, log_sum_norm)
    kv, attend, low, term_far, term_near, *far = lax.optimization_barrier(
        (kv, attend, low, term_far, term_near, *far)
    )
    rows = over_ctx(back_product(line.astype(jnp.int32).reshape(1), slot_grads, near, far))
    mix = mix_matrix(routes, gates, experts, capacity)

    def x_sum(term):
        return lax.psum_scatter(term, "dp", scatter_dimension=0, tiled=True, axis_index_groups=X_GROUPS)

    sum_far = other_y(x_sum(term_far))
    sum_near = x_sum(term_near)

    def attention(mix, rows, grad_out, attn_out, attend, low, norms, kv):
        grad_hidden, total = key_value_grads(place, mix, rows, grad_out, attn_out, attend, low, kv)
        parts = over_ctx(total)
        return grad_hidden, query_grads(place, grad_hidden, attn_out, low, norms, kv), parts

    grad_hidden, query_gradient, parts = as_one(
        always, attention, mix, rows, grad_out, attn_out, attend, low, log_sum_norm, kv
    )
    parts, sum_far, sum_near = lax.optimization_barrier((parts, sum_far, sum_near))
    key_gradient, value_gradient, grad_up = final_sums(
        parts.reshape(experts, tokens, PAIR), sum_near, sum_far
    )
    return grad_hidden, query_gradient, key_gradient, value_gradient, grad_up.reshape(up_weight.shape)


def solution(mesh):
    placed = (
        P(("dp", "ctx"), "exp"),
        P(("dp", "ctx"), "exp"),
        P(("dp", "ctx"), "exp"),
        P(("dp", "ctx"), "exp"),
        P("exp", ("dp", "ctx")),
        P(("dp", "ctx"), "exp"),
        P(("dp", "ctx"), None),
        P(("dp", "ctx"), None),
        P("dp", "ctx", None, "exp"),
        P("dp", "ctx", None, None),
        P("ctx", "dp", "exp"),
    )
    return jax.shard_map(
        body,
        mesh=mesh,
        in_specs=placed,
        out_specs=(
            P(("dp", "ctx"), "exp"),
            P(("dp", "ctx"), "exp"),
            P(("dp", "ctx"), "exp"),
            P(("dp", "ctx"), "exp"),
            P("ctx", "dp", "exp"),
        ),
        check_vma=False,
    )
```

```python
import functools

import jax
import jax.numpy as jnp
from jax import lax
from jax.experimental import pallas as pl
from jax.experimental.pallas import tpu as pltpu
from jax.sharding import PartitionSpec as P

HEAD_WIDTH = 64
PAIR = 2 * HEAD_WIDTH
KEY_TILE = 512
ROW_TILE = 1024
QUERY_ROW_TILE = 512
X_RING = 4
F32 = jnp.float32
BF16 = jnp.bfloat16

NT = (((1,), (1,)), ((), ()))
TN = (((0,), (0,)), ((), ()))
LIGHT = pl.CostEstimate(flops=1 << 20, bytes_accessed=1 << 16, transcendentals=0)
X_GROUPS = [[0, 1, 2, 3], [4, 5, 6, 7]]


def other_y(shard):
    return lax.ppermute(shard, "dp", [(i, (i + X_RING) % (2 * X_RING)) for i in range(2 * X_RING)])


def run_copies(pairs, sems):
    copies = [pltpu.make_async_copy(src, dst, sems.at[i]) for i, (src, dst) in enumerate(pairs)]
    for copy in copies:
        copy.start()
    return copies


def along_x(shard, by):
    order = [(i, i // X_RING * X_RING + (i + by) % X_RING) for i in range(2 * X_RING)]
    return lax.ppermute(shard, "dp", order)


def x_pieces(shard):
    return [shard] + [along_x(shard, by) for by in range(1, X_RING)]


def back_kernel(line_ref, grads_ref, near_ref, *rest):
    far, (out_ref, grads, weight, back, sems) = rest[:X_RING], rest[X_RING:]
    x, y = line_ref[0] % X_RING, line_ref[0] // X_RING
    half, rows = near_ref.shape[0], far[0].shape[0]
    pieces = [(near_ref, y * half, half)]
    for by, ref in enumerate(far):
        pieces.append((ref, (1 - y) * half + (x + X_RING - by) % X_RING * rows, rows))
    width = out_ref.shape[1] // 2
    sides = [slice(i * width, (i + 1) * width) for i in range(2)]
    arriving, used = [], 1
    copies = run_copies([(grads_ref, grads)], sems)
    for at in sides:
        pairs = [
            (ref.at[:, at], weight.at[pl.ds(pl.multiple_of(start, rows), size), at])
            for ref, start, size in pieces
        ]
        arriving.append(run_copies(pairs, sems.at[pl.ds(used, len(pairs))]))
        used += len(pairs)
    copies[0].wait()
    leaving = []
    for i, at in enumerate(sides):
        for copy in arriving[i]:
            copy.wait()
        back[:, at] = jnp.dot(grads[...], weight[:, at], preferred_element_type=F32).astype(BF16)
        leaving += run_copies([(back.at[:, at], out_ref.at[:, at])], sems.at[pl.ds(used + i, 1)])
    for copy in leaving:
        copy.wait()


def back_product(line, grads, near, far):
    depth, width = grads.shape[1], near.shape[1]
    anywhere = pl.BlockSpec(memory_space=pl.ANY)
    return pl.pallas_call(
        back_kernel,
        out_shape=jax.ShapeDtypeStruct((grads.shape[0], width), BF16),
        in_specs=[pl.BlockSpec(memory_space=pltpu.SMEM)] + [anywhere] * (2 + X_RING),
        out_specs=anywhere,
        scratch_shapes=[
            pltpu.VMEM(grads.shape, BF16),
            pltpu.VMEM((depth, width), BF16),
            pltpu.VMEM((grads.shape[0], width), BF16),
            pltpu.SemaphoreType.DMA((1 + 2 * (1 + X_RING) + 2,)),
        ],
        compiler_params=pltpu.CompilerParams(vmem_limit_bytes=60 * 2**20),
        cost_estimate=LIGHT,
        name="back_rows",
    )(line, grads, near, *far)


def over_ctx(shard):
    return lax.all_to_all(shard, "ctx", 0, 0, tiled=True)


def swap_halves(pair):
    return pltpu.roll(pair, HEAD_WIDTH, 1)


def tile_rows(index, size):
    return pl.ds(pl.multiple_of(index * size, size), size)


def last_tile(place, size, tokens):
    return place * tokens // size


def per_head(pair, tokens):
    even = slice(2 * pair * tokens, (2 * pair + 1) * tokens)
    odd = slice((2 * pair + 1) * tokens, (2 * pair + 2) * tokens)
    return slice(pair * PAIR, (pair + 1) * PAIR), even, odd


def attend_kernel(place_ref, query_ref, norm_ref, kv_ref, attend_ref, low_ref, low, norm):
    tokens, width = query_ref.shape
    j, place = pl.program_id(0), place_ref[0]
    last = last_tile(place, KEY_TILE, tokens)

    @pl.when(j == 0)
    def _():
        first = lax.broadcasted_iota(jnp.int32, (tokens, PAIR), 1) < HEAD_WIDTH
        for pair in range(width // PAIR):
            columns, even, odd = per_head(pair, tokens)
            q = query_ref[:, columns].astype(F32) * (HEAD_WIDTH**-0.5)
            low[even, :] = jnp.where(first, q, 0.0).astype(BF16)
            low[odd, :] = jnp.where(first, swap_halves(q), 0.0).astype(BF16)
            norm[:, even] = norm_ref[2 * pair : 2 * pair + 1, :]
            norm[:, odd] = norm_ref[2 * pair + 1 : 2 * pair + 2, :]
        low_ref[...] = low[...]

    def tile(masked):
        kv = kv_ref[tile_rows(j, KEY_TILE), :]
        for r in range(low.shape[0] // ROW_TILE):
            at = slice(r * ROW_TILE, (r + 1) * ROW_TILE)
            scores = lax.dot_general(kv, low[at, :], NT, preferred_element_type=F32)
            attend = jnp.exp(scores - norm[:, at])
            if masked:
                key_pos = j * KEY_TILE + lax.broadcasted_iota(jnp.int32, attend.shape, 0)
                token = lax.broadcasted_iota(jnp.int32, attend.shape, 1) % tokens
                attend = jnp.where(key_pos <= place * tokens + token, attend, 0.0)
            attend_ref[:, at] = attend.astype(BF16)

    pl.when(j < last)(lambda: tile(False))
    pl.when(j == last)(lambda: tile(True))


def key_value_kernel(
    place_ref, mix_ref, rows_ref, grad_out_ref, out_ref, attend_ref, low_ref, kv_ref,
    hidden_ref, sum_ref, high, delta, held, sems,
):
    tokens, width = grad_out_ref.shape
    last = last_tile(place_ref[0], KEY_TILE, tokens)

    def fetch(j):
        return pltpu.make_async_copy(attend_ref.at[tile_rows(j, KEY_TILE)], held.at[j], sems.at[j])

    def ahead(j, carry):
        fetch(j).start()
        return carry

    def prepare():
        first = lax.broadcasted_iota(jnp.int32, (tokens, PAIR), 1) < HEAD_WIDTH
        mixed = jnp.dot(mix_ref[...], rows_ref[...], preferred_element_type=F32)
        hidden = (
            grad_out_ref[...].astype(F32)
            + (mixed[:tokens] + (mixed[tokens : 2 * tokens] + mixed[2 * tokens :]))
        ).astype(BF16)
        hidden_ref[...] = hidden
        for pair in range(width // PAIR):
            columns, even, odd = per_head(pair, tokens)
            g = hidden[:, columns].astype(F32)
            high[even, :] = jnp.where(first, 0.0, swap_halves(g)).astype(BF16)
            high[odd, :] = jnp.where(first, 0.0, g).astype(BF16)
            prod = (g * out_ref[:, columns].astype(F32)).T
            delta[:, even] = jnp.sum(prod[:HEAD_WIDTH], axis=0, keepdims=True)
            delta[:, odd] = jnp.sum(prod[HEAD_WIDTH:], axis=0, keepdims=True)

    lax.fori_loop(0, last + 1, ahead, 0)
    prepare()

    def tile(j, carry):
        fetch(j).wait()
        kv = kv_ref[tile_rows(j, KEY_TILE), :]
        total = jnp.zeros((KEY_TILE, PAIR), F32)
        for r in range(high.shape[0] // ROW_TILE):
            at = slice(r * ROW_TILE, (r + 1) * ROW_TILE)
            g = high[at, :]
            attend = held[j, :, at]
            prob = lax.dot_general(kv, g, NT, preferred_element_type=F32)
            score_grad = (attend.astype(F32) * (prob - delta[:, at])).astype(BF16)
            total = total + jnp.dot(score_grad, low_ref[at, :], preferred_element_type=F32)
            total = total + jnp.dot(attend, g, preferred_element_type=F32)
        sum_ref[tile_rows(j, KEY_TILE), :] = total.astype(BF16)
        return carry

    def empty(j, carry):
        sum_ref[tile_rows(j, KEY_TILE), :] = jnp.zeros((KEY_TILE, PAIR), BF16)
        return carry

    lax.fori_loop(0, last + 1, tile, 0)
    lax.fori_loop(last + 1, kv_ref.shape[0] // KEY_TILE, empty, 0)


def query_kernel(
    place_ref, hidden_ref, out_ref, low_ref, norm_ref, kv_ref, grad_ref, high, norm, delta, total
):
    tokens, width = hidden_ref.shape
    j, place = pl.program_id(0), place_ref[0]
    last = last_tile(place, KEY_TILE, tokens)
    first = lax.broadcasted_iota(jnp.int32, (tokens, PAIR), 1) < HEAD_WIDTH

    @pl.when(j == 0)
    def _():
        norms = norm_ref[...].T
        for pair in range(width // PAIR):
            columns, even, odd = per_head(pair, tokens)
            g = hidden_ref[:, columns].astype(F32)
            high[even, :] = jnp.where(first, 0.0, swap_halves(g)).astype(BF16)
            high[odd, :] = jnp.where(first, 0.0, g).astype(BF16)
            prod = g * out_ref[:, columns].astype(F32)
            delta[even, :] = jnp.sum(jnp.where(first, prod, 0.0), axis=1, keepdims=True)
            delta[odd, :] = jnp.sum(jnp.where(first, 0.0, prod), axis=1, keepdims=True)
            norm[even, :] = norms[:, 2 * pair : 2 * pair + 1]
            norm[odd, :] = norms[:, 2 * pair + 1 : 2 * pair + 2]
        total[...] = jnp.zeros_like(total)

    def tile(masked):
        kv = kv_ref[tile_rows(j, KEY_TILE), :]
        for r in range(high.shape[0] // QUERY_ROW_TILE):
            at = slice(r * QUERY_ROW_TILE, (r + 1) * QUERY_ROW_TILE)
            scores = lax.dot_general(low_ref[at, :], kv, NT, preferred_element_type=F32)
            attend = jnp.exp(scores - norm[at, :])
            if masked:
                key_pos = j * KEY_TILE + lax.broadcasted_iota(jnp.int32, attend.shape, 1)
                token = lax.broadcasted_iota(jnp.int32, attend.shape, 0) % tokens
                attend = jnp.where(key_pos <= place * tokens + token, attend, 0.0)
            prob = lax.dot_general(high[at, :], kv, NT, preferred_element_type=F32)
            score_grad = (attend * (prob - delta[at, :])).astype(BF16)
            total[at, :] += jnp.dot(score_grad, kv, preferred_element_type=F32)

    pl.when(j < last)(lambda: tile(False))
    pl.when(j == last)(lambda: tile(True))

    @pl.when(j == pl.num_programs(0) - 1)
    def _():
        for pair in range(width // PAIR):
            columns, even, odd = per_head(pair, tokens)
            both = jnp.where(first, total[even, :], swap_halves(total[odd, :]))
            grad_ref[:, columns] = (both * (HEAD_WIDTH**-0.5)).astype(BF16)


def whole(array):
    return pl.BlockSpec(array.shape, lambda j, place: (0, 0))


def call(kernel, name, steps, in_specs, out_specs, out_shape, scratch, matmuls, elements, place, *operands):
    return pl.pallas_call(
        kernel,
        out_shape=out_shape,
        grid_spec=pltpu.PrefetchScalarGridSpec(
            num_scalar_prefetch=1,
            grid=(steps,),
            in_specs=in_specs,
            out_specs=out_specs,
            scratch_shapes=scratch,
        ),
        compiler_params=pltpu.CompilerParams(vmem_limit_bytes=60 * 2**20),
        cost_estimate=LIGHT,
        name=name,
    )(place, *operands)


def attend_block(tokens):
    return lambda j, place: (jnp.minimum(j, last_tile(place[0], KEY_TILE, tokens)), 0)


def attention_weights(place, queries, norms, kv):
    tokens, width = queries.shape
    keys, rows = kv.shape[0], width // HEAD_WIDTH * tokens
    out = (jax.ShapeDtypeStruct((keys, rows), BF16), jax.ShapeDtypeStruct((rows, PAIR), BF16))
    return call(
        attend_kernel,
        "attend",
        keys // KEY_TILE,
        [whole(queries), whole(norms), whole(kv)],
        (pl.BlockSpec((KEY_TILE, rows), attend_block(tokens)), whole(out[1])),
        out,
        [pltpu.VMEM((rows, PAIR), BF16), pltpu.VMEM((1, rows), F32)],
        1,
        keys * rows,
        place,
        queries,
        norms,
        kv,
    )


def key_value_grads(place, mix, rows, grad_out, attn_out, attend, low, kv):
    tokens, width = grad_out.shape
    keys, lines = attend.shape
    out = (jax.ShapeDtypeStruct((tokens, width), BF16), jax.ShapeDtypeStruct((keys, PAIR), BF16))
    return call(
        key_value_kernel,
        "key_value_grads",
        1,
        [whole(mix), whole(rows), whole(grad_out), whole(attn_out)]
        + [pl.BlockSpec(memory_space=pl.ANY), whole(low), whole(kv)],
        (whole(out[0]), whole(out[1])),
        out,
        [
            pltpu.VMEM((lines, PAIR), BF16),
            pltpu.VMEM((1, lines), F32),
            pltpu.VMEM((keys // KEY_TILE, KEY_TILE, lines), BF16),
            pltpu.SemaphoreType.DMA((keys // KEY_TILE,)),
        ],
        3,
        keys * lines,
        place,
        mix,
        rows,
        grad_out,
        attn_out,
        attend,
        low,
        kv,
    )


def query_grads(place, hidden, attn_out, low, norms, kv):
    keys, lines = kv.shape[0], low.shape[0]
    out = jax.ShapeDtypeStruct(hidden.shape, BF16)
    return call(
        query_kernel,
        "query_grads",
        keys // KEY_TILE,
        [whole(x) for x in (hidden, attn_out, low, norms, kv)],
        whole(out),
        out,
        [
            pltpu.VMEM((lines, PAIR), BF16),
            pltpu.VMEM((lines, 1), F32),
            pltpu.VMEM((lines, 1), F32),
            pltpu.VMEM((lines, PAIR), F32),
        ],
        3,
        keys * lines,
        place,
        hidden,
        attn_out,
        low,
        norms,
        kv,
    )


def as_one(always, step, *operands):
    out = jax.eval_shape(step, *operands)

    def never(*_):
        return jax.tree.map(lambda x: jnp.zeros(x.shape, x.dtype), out)

    return lax.cond(always, step, never, *operands)


def pack_kernel(key_ref, value_ref, kv_ref):
    tokens = key_ref.shape[1]
    keys, values = key_ref[...].astype(F32).T.astype(BF16), value_ref[...].astype(F32).T.astype(BF16)
    for i in range(kv_ref.shape[0] // tokens):
        kv_ref[i * tokens : (i + 1) * tokens, :HEAD_WIDTH] = keys
        kv_ref[i * tokens : (i + 1) * tokens, HEAD_WIDTH:] = values


def packed(keys, values):
    chips = lax.axis_size("ctx") // 2
    vmem = pl.BlockSpec(memory_space=pltpu.VMEM)
    return pl.pallas_call(
        pack_kernel,
        out_shape=jax.ShapeDtypeStruct((chips * keys.shape[0], PAIR), BF16),
        in_specs=[vmem] * 2,
        out_specs=vmem,
        cost_estimate=LIGHT,
        name="pack",
    )(keys.T, values.T)


def over_chips(copies):
    chips = lax.axis_size("ctx") // 2
    same_core = [[2 * i + core for i in range(chips)] for core in range(2)]
    return lax.all_to_all(copies, "ctx", 0, 0, tiled=True, axis_index_groups=same_core)


def with_other_core(mine):
    devices = lax.axis_size("ctx")
    theirs = lax.ppermute(mine, "ctx", [(i, i ^ 1) for i in range(devices)])
    first = lax.axis_index("ctx") % 2 == 0
    parts = [x.reshape(devices // 2, -1, PAIR) for x in (mine, theirs)]
    both = jnp.stack([jnp.where(first, parts[0], parts[1]), jnp.where(first, parts[1], parts[0])], axis=1)
    return both.reshape(2 * mine.shape[0], PAIR)


def sum_kernel(parts_ref, near_ref, far_ref, key_ref, value_ref, up_ref):
    total = jnp.sum(parts_ref[...].astype(F32), axis=0).T
    key_ref[...] = total[:HEAD_WIDTH].astype(BF16)
    value_ref[...] = total[HEAD_WIDTH:].astype(BF16)
    up_ref[...] = (near_ref[...].astype(F32) + far_ref[...].astype(F32)).astype(BF16)


def final_sums(parts, near, far):
    vmem = pl.BlockSpec(memory_space=pltpu.VMEM)
    out = jax.ShapeDtypeStruct((HEAD_WIDTH, parts.shape[1]), BF16)
    keys, values, up = pl.pallas_call(
        sum_kernel,
        out_shape=(out, out, jax.ShapeDtypeStruct(near.shape, BF16)),
        in_specs=[vmem] * 3,
        out_specs=(vmem,) * 3,
        compiler_params=pltpu.CompilerParams(vmem_limit_bytes=60 * 2**20),
        cost_estimate=LIGHT,
        name="final_sums",
    )(parts, near, far)
    return keys.T, values.T, up


def mix_matrix(routes, gates, experts, capacity):
    tokens, top = routes.shape
    flat = routes.reshape(-1)
    number = jnp.arange(flat.shape[0], dtype=jnp.int32)
    same = (flat[:, None] == flat[None, :]) & (number[None, :] < number[:, None])
    slots = (flat * capacity + jnp.sum(same.astype(jnp.int32), axis=1)).reshape(tokens, top)
    terms, left = [], gates
    for _ in range(3):
        term = left.astype(BF16)
        left = left - term.astype(F32)
        terms.append(term)
    columns = jnp.arange(experts * capacity, dtype=jnp.int32)
    hit = slots[:, :, None] == columns[None, None, :]
    return jnp.concatenate(
        [sum(jnp.where(hit[:, k], t[:, k, None], 0).astype(BF16) for k in range(top)) for t in terms], axis=0
    )


def body(
    queries,
    saved_key_rows,
    saved_value_rows,
    attn_out,
    log_sum_norm,
    grad_out,
    routes,
    gates,
    expert_in,
    hidden_grad,
    up_weight,
):
    experts = lax.axis_size("ctx")
    place = lax.axis_index("ctx").astype(jnp.int32).reshape(1)
    line = lax.axis_index("dp")
    x, y = line % X_RING, line // X_RING
    tokens, width = queries.shape
    capacity = hidden_grad.shape[2] // experts
    weight = up_weight[0]
    shard_rows = weight.shape[0]
    half_rows = X_RING * shard_rows

    always = place[0] < experts

    crossed = other_y(weight)
    near = lax.all_gather(weight, "dp", axis=0, tiled=True, axis_index_groups=X_GROUPS)
    slot_grads = hidden_grad[0, 0]

    def first(keys, values, grads, inputs):
        def weight_term(half):
            part = lax.dynamic_slice_in_dim(grads, half * half_rows, half_rows, 1)
            return lax.dot_general(part, inputs, TN, preferred_element_type=F32).astype(BF16)

        return packed(keys, values), weight_term(1 - y), weight_term(y)

    kv, term_far, term_near = as_one(
        always, first, saved_key_rows, saved_value_rows, slot_grads, expert_in[0, 0]
    )
    kv = over_chips(kv)
    crossed, routes, term_far, term_near = lax.optimization_barrier((crossed, routes, term_far, term_near))
    far = x_pieces(crossed)

    def second(kv, queries, norms):
        kv = with_other_core(kv)
        return kv, *attention_weights(place, queries, norms, kv)

    kv, attend, low = as_one(always, second, kv, queries, log_sum_norm)
    kv, attend, low, term_far, term_near, *far = lax.optimization_barrier(
        (kv, attend, low, term_far, term_near, *far)
    )
    rows = over_ctx(back_product(line.astype(jnp.int32).reshape(1), slot_grads, near, far))
    mix = mix_matrix(routes, gates, experts, capacity)

    def x_sum(term):
        return lax.psum_scatter(term, "dp", scatter_dimension=0, tiled=True, axis_index_groups=X_GROUPS)

    sum_far = other_y(x_sum(term_far))
    sum_near = x_sum(term_near)

    def attention(mix, rows, grad_out, attn_out, attend, low, norms, kv):
        grad_hidden, total = key_value_grads(place, mix, rows, grad_out, attn_out, attend, low, kv)
        parts = over_ctx(total)
        return grad_hidden, query_grads(place, grad_hidden, attn_out, low, norms, kv), parts

    grad_hidden, query_gradient, parts = as_one(
        always, attention, mix, rows, grad_out, attn_out, attend, low, log_sum_norm, kv
    )
    parts, sum_far, sum_near = lax.optimization_barrier((parts, sum_far, sum_near))
    key_gradient, value_gradient, grad_up = final_sums(
        parts.reshape(experts, tokens, PAIR), sum_near, sum_far
    )
    return grad_hidden, query_gradient, key_gradient, value_gradient, grad_up.reshape(up_weight.shape)


def solution(mesh):
    placed = (
        P(("dp", "ctx"), "exp"),
        P(("dp", "ctx"), "exp"),
        P(("dp", "ctx"), "exp"),
        P(("dp", "ctx"), "exp"),
        P("exp", ("dp", "ctx")),
        P(("dp", "ctx"), "exp"),
        P(("dp", "ctx"), None),
        P(("dp", "ctx"), None),
        P("dp", "ctx", None, "exp"),
        P("dp", "ctx", None, None),
        P("ctx", "dp", "exp"),
    )
    return jax.shard_map(
        body,
        mesh=mesh,
        in_specs=placed,
        out_specs=(
            P(("dp", "ctx"), "exp"),
            P(("dp", "ctx"), "exp"),
            P(("dp", "ctx"), "exp"),
            P(("dp", "ctx"), "exp"),
            P("ctx", "dp", "exp"),
        ),
        check_vma=False,
    )
```
